32 devices in a mesh: row: 2 (over y), col: 4 (over x, core), dp: 4 (over z).
Axes of the slice: x: 2, y: 2, z: 4, core: 2. Of those that a mesh axis runs over, the one named last changes fastest.
Arguments:
- image: bfloat16 [4, 256, 48, 512], P('dp', None, 'row', 'col'), may hold values from -6 to 6
- labels: int32 [4, 2, 8], P('dp', 'row', 'col'), may hold values from 0 to 7
- weights: float32 [141312], replicated, may hold values from -0.375 to 0.375
- momentum: float32 [141312], P(('row', 'col', 'dp')), may hold values from -0.006 to 0.006
Outputs:
- new_weights: float32 [141312], P(('row', 'col', 'dp'))
- new_momentum: float32 [141312], P(('row', 'col', 'dp'))
- update: float32 [141312], P(('row', 'col', 'dp'))
- loss: float32 [], replicated
The draws below stay inside these ranges and needn't reach their ends.
All inputs are finite; a program needn't handle non-finite values. Where the reference program divides by a largest or mean magnitude, that divisor is 1e-20 or more.
Results may differ from the reference program's by a relative error of at most 0.0011.
Values may be sent and summed in bfloat16 or wider, within the bound.
A program may use at most 64 MiB of HBM per device.

```python
import jax
import jax.numpy as jnp
from jax import lax

C = 256
MID = 64
CLASSES = 8
TILE_ROWS = 24
TILE_COLS = 64
SLIDES = 4
NR = 48
NC = 512
PARAM = 141312
NTILES = 64


def set_ends(values, rng, smallest, largest):
    dims = values.shape
    place = [jax.random.randint(jax.random.fold_in(rng, axis), (), 0, dims[axis]) for axis in range(len(dims))]
    values = values.at[tuple(place)].set(smallest)
    longest = dims.index(max(dims))
    place[longest] = (place[longest] + 1) % dims[longest]
    return values.at[tuple(place)].set(largest)


def block_levels(own_key, extent, pieces, low, largest):
    loudness, own = 1.0, jax.random.fold_in(own_key, 6)
    for dim, shards_of in pieces:
        steps = jnp.exp(jax.random.uniform(jax.random.fold_in(own, dim), (shards_of,), jnp.float32, low / len(pieces), largest / len(pieces)))
        loudness = loudness * jnp.repeat(steps, extent[dim] // shards_of).reshape([-1 if axis == dim else 1 for axis in range(len(extent))])
    return loudness


def scatter_about(own_key, dims, spread, most, split=(), kind=jnp.bfloat16):
    drawn = jax.random.normal(own_key, dims, jnp.float32) * spread
    if len(split) > 0:
        drawn = block_levels(own_key, dims, split, -0.22, 0.18) * drawn
    return jnp.clip(drawn, min=-most, max=most).astype(kind)


def setup_inputs(seed: int = 0) -> dict:
    seeds = jax.random.split(jax.random.key(seed), 5)
    image = scatter_about(seeds[0], (SLIDES, C, NR, NC), 1.0, 6.0, ((0, 4), (2, 2), (3, 4)))
    labels = set_ends(jax.random.randint(seeds[1], (SLIDES, NR // TILE_ROWS, NC // TILE_COLS), 0, CLASSES), jax.random.fold_in(seeds[1], 1), 0, CLASSES - 1).astype(jnp.int32)
    weights = scatter_about(seeds[2], (PARAM,), C ** -0.5, 0.375, (), jnp.float32)
    momentum = scatter_about(seeds[3], (PARAM,), 0.001, 0.006, ((0, 32),), jnp.float32)
    return dict(image=image, labels=labels, weights=weights, momentum=momentum)


beta_one = 0.9
beta_two = 0.99
learn_rate = 0.0001
weight_decay = 0.1


def product(spec, left, right):
    return jnp.einsum(spec, left.astype(jnp.float32), right.astype(jnp.float32), precision=lax.Precision.HIGHEST)


def unpack(weights):
    offset = 0
    blocks_list = []
    for number in range(2):
        w_in = weights[offset:offset + C * MID].reshape(C, MID)
        offset = offset + C * MID
        w_mid = weights[offset:offset + 9 * MID * MID].reshape(9, MID, MID)
        offset = offset + 9 * MID * MID
        w_out = weights[offset:offset + MID * C].reshape(MID, C)
        offset = offset + MID * C
        blocks_list.append((w_in.astype(jnp.bfloat16), w_mid.astype(jnp.bfloat16), w_out.astype(jnp.bfloat16)))
    head = weights[offset:].reshape(C, CLASSES)
    return blocks_list, head


def border(field):
    return jnp.pad(field, ((0, 0), (1, 1), (1, 1)))


def conv_taps(w_mid, padded, height, width):
    total = jnp.zeros((w_mid.shape[2], height, width), jnp.float32)
    for position in range(9):
        shift_row = position // 3
        shift_col = position % 3
        total = total + product('io,ihw->ohw', w_mid[position], padded[:, shift_row:shift_row + height, shift_col:shift_col + width])
    return total


def slide_terms(slide, label_grid, blocks_list, head):
    height, width = slide.shape[1], slide.shape[2]
    stored = []
    inputs = slide
    for w_in, w_mid, w_out in blocks_list:
        h_first = jnp.maximum(product('io,ihw->ohw', w_in, inputs), 0.0).astype(jnp.bfloat16)
        padded = border(h_first)
        h_second = jnp.maximum(conv_taps(w_mid, padded, height, width), 0.0).astype(jnp.bfloat16)
        output = jnp.maximum(product('io,ihw->ohw', w_out, h_second) + inputs.astype(jnp.float32), 0.0).astype(jnp.bfloat16)
        stored.append((inputs, padded, h_second, output))
        inputs = output
    tiles_a = height // TILE_ROWS
    tiles_b = width // TILE_COLS
    pooled = jnp.mean(inputs.astype(jnp.float32).reshape(C, tiles_a, TILE_ROWS, tiles_b, TILE_COLS), axis=(2, 4))
    logits = product('cab,ck->abk', pooled, head)
    highest = jnp.max(logits, axis=-1, keepdims=True)
    logsum = jnp.log(jnp.sum(jnp.exp(logits - highest), axis=-1, keepdims=True)) + highest
    onehot = (label_grid[:, :, None] == jnp.arange(CLASSES, dtype=jnp.int32)).astype(jnp.float32)
    loss_sum = jnp.sum(logsum[:, :, 0] - jnp.sum(onehot * logits, axis=-1))
    dlogits = (jnp.exp(logits - logsum) - onehot) / NTILES
    grad_head = product('cab,abk->ck', pooled, dlogits)
    dpooled = product('abk,ck->cab', dlogits, head) / (TILE_ROWS * TILE_COLS)
    upstream = jnp.broadcast_to(dpooled[:, :, None, :, None], (C, tiles_a, TILE_ROWS, tiles_b, TILE_COLS)).reshape(C, height, width).astype(jnp.bfloat16)
    grads = [None, None]
    for number in (1, 0):
        w_in, w_mid, w_out = blocks_list[number]
        inputs, padded, h_second, output = stored[number]
        d_sum = jnp.where(output > 0, upstream, jnp.zeros_like(upstream)).astype(jnp.bfloat16)
        grad_out = product('ihw,ohw->io', h_second, d_sum)
        d_second = product('io,ohw->ihw', w_out, d_sum)
        d_second = jnp.where(h_second > 0, d_second, 0.0).astype(jnp.bfloat16)
        grad_mid = jnp.stack([product('ihw,ohw->io', padded[:, position // 3:position // 3 + height, position % 3:position % 3 + width], d_second) for position in range(9)])
        spread_back = border(d_second)
        d_first = jnp.zeros((MID, height, width), jnp.float32)
        for position in range(9):
            shift_row = 2 - position // 3
            shift_col = 2 - position % 3
            d_first = d_first + product('io,ohw->ihw', w_mid[position], spread_back[:, shift_row:shift_row + height, shift_col:shift_col + width])
        h_first = padded[:, 1:-1, 1:-1]
        d_first = jnp.where(h_first > 0, d_first, 0.0).astype(jnp.bfloat16)
        grad_in = product('ihw,ohw->io', inputs, d_first)
        if number == 1:
            upstream = (product('io,ohw->ihw', w_in, d_first) + d_sum.astype(jnp.float32)).astype(jnp.bfloat16)
        grads[number] = jnp.concatenate([grad_in.ravel(), grad_mid.ravel(), grad_out.ravel()])
    flat = jnp.concatenate([grads[0], grads[1], grad_head.ravel()])
    return flat, loss_sum


def reference(image, labels, weights, momentum):
    blocks_list, head = unpack(weights)

    def per_slide(pair):
        return slide_terms(pair[0], pair[1], blocks_list, head)

    flats, losses = lax.map(per_slide, (image, labels))
    grad = jnp.sum(flats, axis=0)
    loss = jnp.sum(losses) / NTILES
    mixed = beta_one * momentum + (1.0 - beta_one) * grad
    scale_tau = jnp.mean(jnp.abs(mixed)) + 1e-6
    update = mixed / (jnp.abs(mixed) + scale_tau)
    new_weights = weights - learn_rate * (update + weight_decay * weights)
    new_momentum = beta_two * momentum + (1.0 - beta_two) * grad
    return new_weights, new_momentum, update, loss
```

```python
import jax
import jax.numpy as jnp
from jax import lax
from jax.experimental import pallas as pl
from jax.experimental.pallas import tpu as pltpu
from jax.sharding import PartitionSpec as P

C = 256
MID = 64
CLASSES = 8
TILE_ROWS = 24
TILE_COLS = 64


beta_one = 0.9
beta_two = 0.99
learn_rate = 0.0001
weight_decay = 0.1


def extended(block, sides, width):
    for axis, dim in sides:
        count = lax.axis_size(axis)
        forward = [(i, i + 1) for i in range(count - 1)]
        backward = [(target, source) for source, target in forward]
        low = lax.ppermute(
            lax.slice_in_dim(block, block.shape[dim] - width, None, axis=dim), axis, forward
        )
        high = lax.ppermute(lax.slice_in_dim(block, 0, width, axis=dim), axis, backward)
        block = jnp.concatenate([low, block, high], axis=dim)
    return block


def unpack(weights):
    offset = 0
    blocks_list = []
    for number in range(2):
        w_in = weights[offset : offset + C * MID].reshape(C, MID)
        offset = offset + C * MID
        w_mid = weights[offset : offset + 9 * MID * MID].reshape(9, MID, MID)
        offset = offset + 9 * MID * MID
        w_out = weights[offset : offset + MID * C].reshape(MID, C)
        offset = offset + MID * C
        blocks_list.append(
            (w_in.astype(jnp.bfloat16), w_mid.astype(jnp.bfloat16), w_out.astype(jnp.bfloat16))
        )
    head = weights[offset:].reshape(C, CLASSES)
    return (blocks_list, head)


def forward_rim(field):
    return extended(field, (("row", 1), ("col", 2)), 1)


def backward_rim(field):
    return extended(field, (("row", 1), ("col", 2)), 1)


def conv_taps(w_mid, padded, height, width):
    total = jnp.zeros((w_mid.shape[2], height, width), jnp.float32)
    for position in range(9):
        shift_row = position // 3
        shift_col = position % 3
        total = total + jnp.einsum(
            "io,ihw->ohw",
            w_mid[position],
            padded[:, shift_row : shift_row + height, shift_col : shift_col + width],
            preferred_element_type=jnp.float32,
        )
    return total


MESH_ID = pl.DeviceIdType.MESH
AXES = ("row", "col", "dp")


def share_rows(share, count):
    first = [d * share // 128 for d in range(count)]
    last = [-(-(d + 1) * share // 128) for d in range(count)]
    return max(b - a for a, b in zip(first, last))


def split_col(ncol):
    return 2 if ncol % 2 == 0 else 1


def peers(sizes):
    nrow, ncol, ndp = sizes
    row, col, dp = (lax.axis_index(a) for a in AXES)

    def plane(k):
        place = lax.rem(row * ncol + col + k, nrow * ncol)
        return (place // ncol, lax.rem(place, ncol), dp)

    def line(k):
        return (row, col, lax.rem(dp + k, ndp))

    return plane, line


def greet(sizes):
    nrow, ncol, ndp = sizes
    plane, line = peers(sizes)
    barrier = pltpu.get_barrier_semaphore()
    for target, count in ((plane, nrow * ncol), (line, ndp)):
        def one(k, carry, target=target):
            pl.semaphore_signal(barrier, inc=1, device_id=target(k), device_id_type=MESH_ID)
            return carry
        lax.fori_loop(1, count, one, 0)
    pl.semaphore_wait(barrier, nrow * ncol - 1 + ndp - 1)


def exchange(count, source, landing, target, send, recv):
    def copy(k):
        return pltpu.make_async_remote_copy(
            src_ref=source(k), dst_ref=landing.at[k - 1], send_sem=send.at[k - 1],
            recv_sem=recv.at[k - 1], device_id=target(k), device_id_type=MESH_ID)

    def start(k, carry):
        copy(k).start()
        return carry

    def finish(k, carry):
        copy(k).wait()
        return carry

    lax.fori_loop(1, count, start, 0)
    lax.fori_loop(1, count, finish, 0)


def lion_kernel(sizes, share, params, flat_ref, loss_ref, mom_ref, wgt_ref, out_ref, total_ref,
                held, a1, r1, a2, r2, a3, r3, r4, mine, rp, line_sum, rl, *sems):
    nrow, ncol, ndp = sizes
    lo_n = split_col(ncol)
    hi_n = ncol // lo_n
    rows = mom_ref.shape[0]
    row, col, dp = (lax.axis_index(a) for a in AXES)
    lo, hi = lax.rem(col, lo_n), col // lo_n
    greet(sizes)
    for r in range(nrow):
        for c in range(ncol):
            for z in range(ndp):
                start = ((r * ncol + c) * ndp + z) * share // 128
                have = min(rows, flat_ref.shape[0] - start)
                held[c % lo_n, r, c // lo_n, z, 0:have] = flat_ref[start : start + have, :]

    def step(count, me, now, landing, later, where, send, recv):
        exchange(count, lambda k: now.at[lax.rem(me + k, count)], landing,
                 lambda k: where(lax.rem(me + k, count)), send, recv)
        total = now[me]
        for k in range(count - 1):
            total = total + landing[k]
        if later is None:
            return total
        later[...] = total

    step(lo_n, lo, held, r1, a1, lambda p: (row, hi * lo_n + p, dp), sems[0], sems[1])
    step(nrow, row, a1, r2, a2, lambda p: (p, col, dp), sems[2], sems[3])
    step(hi_n, hi, a2, r3, a3, lambda p: (row, p * lo_n + lo, dp), sems[4], sems[5])
    grad = step(ndp, dp, a3, r4, None, lambda p: (row, col, p), sems[6], sems[7])

    me = (row * ncol + col) * ndp + dp
    skip = lax.rem(me * share, 128)
    place = (lax.broadcasted_iota(jnp.int32, (rows, 128), 0) * 128
             + lax.broadcasted_iota(jnp.int32, (rows, 128), 1))
    inside = jnp.logical_and(place >= skip, place < skip + share)
    momentum = mom_ref[...]
    weight = wgt_ref[...]
    mixed = beta_one * momentum + (1.0 - beta_one) * grad
    size = jnp.abs(mixed)
    part = jnp.sum(jnp.where(inside, size, 0.0), axis=0, keepdims=True)
    which = lax.broadcasted_iota(jnp.int32, (8, 128), 0)
    mine[...] = jnp.where(which == 0, part, jnp.where(which == 1, loss_ref[...], 0.0))
    plane, line = peers(sizes)
    exchange(nrow * ncol, lambda k: mine, rp, plane, sems[8], sems[9])
    total = mine[...]
    for k in range(nrow * ncol - 1):
        total = total + rp[k]
    line_sum[...] = total
    exchange(ndp, lambda k: line_sum, rl, line, sems[10], sems[11])
    for k in range(ndp - 1):
        total = total + rl[k]
    total_ref[...] = jnp.broadcast_to(jnp.sum(total, axis=1, keepdims=True), (8, 128))
    tau = jnp.sum(total[0:1, :], axis=1, keepdims=True) / params + 1e-06
    update = mixed / (size + tau)
    out_ref[0] = weight - learn_rate * (update + weight_decay * weight)
    out_ref[1] = beta_two * momentum + (1.0 - beta_two) * grad
    out_ref[2] = update


def lion_step(flat, loss_part, weights, momentum):
    sizes = tuple(lax.axis_size(a) for a in AXES)
    nrow, ncol, ndp = sizes
    count = nrow * ncol * ndp
    share = momentum.shape[0]
    params = weights.shape[0]
    rows = share_rows(share, count)
    me = lax.axis_index(AXES)
    skip = me * share % 128
    first = me * share // 128
    mom = lax.dynamic_update_slice(jnp.zeros((rows * 128,), jnp.float32), momentum, (skip,))
    spare = max(0, (count - 1) * share // 128 + rows - params // 128)
    wgt = jnp.pad(weights.reshape(-1, 128), ((0, spare), (0, 0)))
    wgt = lax.dynamic_slice_in_dim(wgt, first, rows, 0)
    lane0 = jnp.arange(128)[None, :] == 0
    loss_row = jnp.where(lane0, loss_part, 0.0)
    lo_n = split_col(ncol)
    hi_n = ncol // lo_n
    f32 = jnp.float32
    tail = (rows, 128)
    plane_n = nrow * ncol
    counts = (lo_n, nrow, hi_n, ndp, plane_n, ndp)
    sems = [pltpu.SemaphoreType.DMA((max(n - 1, 1),)) for n in counts for _ in range(2)]
    vmem = pl.BlockSpec(memory_space=pltpu.VMEM)

    def land(n, *rest):
        return pltpu.VMEM((max(n - 1, 1),) + rest + tail, f32)

    out, total = pl.pallas_call(
        lambda *refs: lion_kernel(sizes, share, params, *refs),
        out_shape=(jax.ShapeDtypeStruct((3,) + tail, f32), jax.ShapeDtypeStruct((8, 128), f32)),
        in_specs=[vmem] * 4,
        out_specs=(vmem, vmem),
        scratch_shapes=[
            pltpu.VMEM((lo_n, nrow, hi_n, ndp) + tail, f32),
            pltpu.VMEM((nrow, hi_n, ndp) + tail, f32), land(lo_n, nrow, hi_n, ndp),
            pltpu.VMEM((hi_n, ndp) + tail, f32), land(nrow, hi_n, ndp),
            pltpu.VMEM((ndp,) + tail, f32), land(hi_n, ndp),
            land(ndp),
            pltpu.VMEM((8, 128), f32), pltpu.VMEM((max(plane_n - 1, 1), 8, 128), f32),
            pltpu.VMEM((8, 128), f32), pltpu.VMEM((max(ndp - 1, 1), 8, 128), f32),
        ] + sems,
        compiler_params=pltpu.CompilerParams(
            collective_id=0, has_side_effects=True, vmem_limit_bytes=40 * 1024 * 1024),
    )(flat.reshape(-1, 128), loss_row, mom.reshape(rows, 128), wgt)
    out = lax.dynamic_slice_in_dim(out.reshape(3, rows * 128), skip, share, 1)
    return out[0], out[1], out[2], total[1, 0]


def local(image, labels, weights, momentum):
    inputs = image[0]
    label_grid = labels[0]
    height, width = (inputs.shape[1], inputs.shape[2])
    blocks_list, head = unpack(weights)
    total_tiles = (
        label_grid.shape[0]
        * label_grid.shape[1]
        * lax.axis_size("row")
        * lax.axis_size("col")
        * lax.axis_size("dp")
    )
    stored = []
    for w_in, w_mid, w_out in blocks_list:
        h_first = jnp.maximum(
            jnp.einsum("io,ihw->ohw", w_in, inputs, preferred_element_type=jnp.float32), 0.0
        ).astype(jnp.bfloat16)
        padded = forward_rim(h_first)
        h_second = jnp.maximum(conv_taps(w_mid, padded, height, width), 0.0).astype(jnp.bfloat16)
        output = jnp.maximum(
            jnp.einsum("io,ihw->ohw", w_out, h_second, preferred_element_type=jnp.float32)
            + inputs.astype(jnp.float32),
            0.0,
        ).astype(jnp.bfloat16)
        kept = padded
        stored.append((inputs, kept, h_second, output))
        inputs = output
    tiles_a = height // TILE_ROWS
    tiles_b = width // TILE_COLS
    pooled = jnp.mean(
        inputs.astype(jnp.float32).reshape(C, tiles_a, TILE_ROWS, tiles_b, TILE_COLS), axis=(2, 4)
    )
    logits = jnp.einsum("cab,ck->abk", pooled, head, precision=lax.Precision.HIGHEST)
    highest = jnp.max(logits, axis=-1, keepdims=True)
    logsum = jnp.log(jnp.sum(jnp.exp(logits - highest), axis=-1, keepdims=True)) + highest
    onehot = (label_grid[:, :, None] == jnp.arange(CLASSES, dtype=jnp.int32)).astype(jnp.float32)
    loss_part = jnp.sum(logsum[:, :, 0] - jnp.sum(onehot * logits, axis=-1))
    dlogits = (jnp.exp(logits - logsum) - onehot) / total_tiles
    grad_head = jnp.einsum("cab,abk->ck", pooled, dlogits, precision=lax.Precision.HIGHEST)
    dpooled = jnp.einsum("abk,ck->cab", dlogits, head, precision=lax.Precision.HIGHEST) / (
        TILE_ROWS * TILE_COLS
    )
    upstream = (
        jnp.broadcast_to(dpooled[:, :, None, :, None], (C, tiles_a, TILE_ROWS, tiles_b, TILE_COLS))
        .reshape(C, height, width)
        .astype(jnp.bfloat16)
    )
    grads = [None, None]
    for number in (1, 0):
        w_in, w_mid, w_out = blocks_list[number]
        inputs, kept, h_second, output = stored[number]
        padded = kept
        d_sum = jnp.where(output > 0, upstream, jnp.zeros_like(upstream))
        grad_out = jnp.einsum("ihw,ohw->io", h_second, d_sum, preferred_element_type=jnp.float32)
        d_second = jnp.einsum("io,ohw->ihw", w_out, d_sum, preferred_element_type=jnp.float32)
        d_second = jnp.where(h_second > 0, d_second, 0.0).astype(jnp.bfloat16)
        spread_back = backward_rim(d_second)
        grad_mid = jnp.stack(
            [
                jnp.einsum(
                    "ihw,ohw->io",
                    padded[
                        :,
                        position // 3 : position // 3 + height,
                        position % 3 : position % 3 + width,
                    ],
                    d_second,
                    preferred_element_type=jnp.float32,
                )
                for position in range(9)
            ]
        )
        d_first = jnp.zeros((MID, height, width), jnp.float32)
        for position in range(9):
            shift_row = 2 - position // 3
            shift_col = 2 - position % 3
            d_first = d_first + jnp.einsum(
                "io,ohw->ihw",
                w_mid[position],
                spread_back[:, shift_row : shift_row + height, shift_col : shift_col + width],
                preferred_element_type=jnp.float32,
            )
        h_first = padded[:, 1:-1, 1:-1]
        d_first = jnp.where(h_first > 0, d_first, 0.0).astype(jnp.bfloat16)
        grad_in = jnp.einsum("ihw,ohw->io", inputs, d_first, preferred_element_type=jnp.float32)
        if number == 1:
            upstream = (
                jnp.einsum("io,ohw->ihw", w_in, d_first, preferred_element_type=jnp.float32)
                + d_sum.astype(jnp.float32)
            ).astype(jnp.bfloat16)
        grads[number] = jnp.concatenate([grad_in.ravel(), grad_mid.ravel(), grad_out.ravel()])
    flat = jnp.concatenate([grads[0], grads[1], grad_head.ravel()])
    new_weights, new_momentum, update, loss_total = lion_step(flat, loss_part, weights, momentum)
    return (new_weights, new_momentum, update, loss_total / total_tiles)


def solution(mesh):
    in_specs = (P("dp", None, "row", "col"), P("dp", "row", "col"), P(), P(("row", "col", "dp")))
    out_specs = (P(("row", "col", "dp")), P(("row", "col", "dp")), P(("row", "col", "dp")), P())
    return jax.shard_map(local, mesh=mesh, in_specs=in_specs, out_specs=out_specs, check_vma=False)
```

```python
import jax
import jax.numpy as jnp
from jax import lax
from jax.experimental import pallas as pl
from jax.experimental.pallas import tpu as pltpu
from jax.sharding import PartitionSpec as P

C = 256
MID = 64
CLASSES = 8
TILE_ROWS = 24
TILE_COLS = 64


beta_one = 0.9
beta_two = 0.99
learn_rate = 0.0001
weight_decay = 0.1


def unpack(weights):
    offset = 0
    blocks_list = []
    for number in range(2):
        w_in = weights[offset : offset + C * MID].reshape(C, MID)
        offset = offset + C * MID
        w_mid = weights[offset : offset + 9 * MID * MID].reshape(9, MID, MID)
        offset = offset + 9 * MID * MID
        w_out = weights[offset : offset + MID * C].reshape(MID, C)
        offset = offset + MID * C
        blocks_list.append(
            (w_in.astype(jnp.bfloat16), w_mid.astype(jnp.bfloat16), w_out.astype(jnp.bfloat16))
        )
    head = weights[offset:].reshape(C, CLASSES)
    return (blocks_list, head)


MESH_ID = pl.DeviceIdType.MESH
AXES = ("row", "col", "dp")


def share_rows(share, count):
    first = [d * share // 128 for d in range(count)]
    last = [-(-(d + 1) * share // 128) for d in range(count)]
    return max(b - a for a, b in zip(first, last))


def split_col(ncol):
    return 2 if ncol % 2 == 0 else 1


def peers(sizes):
    nrow, ncol, ndp = sizes
    row, col, dp = (lax.axis_index(a) for a in AXES)

    def plane(k):
        place = lax.rem(row * ncol + col + k, nrow * ncol)
        return (place // ncol, lax.rem(place, ncol), dp)

    def line(k):
        return (row, col, lax.rem(dp + k, ndp))

    return plane, line


def greet(sizes):
    nrow, ncol, ndp = sizes
    plane, line = peers(sizes)
    barrier = pltpu.get_barrier_semaphore()
    for target, count in ((plane, nrow * ncol), (line, ndp)):
        def one(k, carry, target=target):
            pl.semaphore_signal(barrier, inc=1, device_id=target(k), device_id_type=MESH_ID)
            return carry
        lax.fori_loop(1, count, one, 0)
    pl.semaphore_wait(barrier, nrow * ncol - 1 + ndp - 1)


def exchange(count, source, landing, target, send, recv):
    def copy(k):
        return pltpu.make_async_remote_copy(
            src_ref=source(k), dst_ref=landing.at[k - 1], send_sem=send.at[k - 1],
            recv_sem=recv.at[k - 1], device_id=target(k), device_id_type=MESH_ID)

    def start(k, carry):
        copy(k).start()
        return carry

    def finish(k, carry):
        copy(k).wait()
        return carry

    lax.fori_loop(1, count, start, 0)
    lax.fori_loop(1, count, finish, 0)


def lion_kernel(sizes, share, params, flat_ref, loss_ref, mom_ref, wgt_ref, out_ref, total_ref,
                held, a1, r1, a2, r2, a3, r3, r4, mine, rp, line_sum, rl, *sems):
    nrow, ncol, ndp = sizes
    lo_n = split_col(ncol)
    hi_n = ncol // lo_n
    rows = mom_ref.shape[0]
    row, col, dp = (lax.axis_index(a) for a in AXES)
    lo, hi = lax.rem(col, lo_n), col // lo_n
    greet(sizes)
    for r in range(nrow):
        for c in range(ncol):
            for z in range(ndp):
                start = ((r * ncol + c) * ndp + z) * share // 128
                have = min(rows, flat_ref.shape[0] - start)
                held[c % lo_n, r, c // lo_n, z, 0:have] = flat_ref[start : start + have, :]

    def step(count, me, now, landing, later, where, send, recv):
        exchange(count, lambda k: now.at[lax.rem(me + k, count)], landing,
                 lambda k: where(lax.rem(me + k, count)), send, recv)
        total = now[me]
        for k in range(count - 1):
            total = total + landing[k]
        if later is None:
            return total
        later[...] = total

    step(lo_n, lo, held, r1, a1, lambda p: (row, hi * lo_n + p, dp), sems[0], sems[1])
    step(nrow, row, a1, r2, a2, lambda p: (p, col, dp), sems[2], sems[3])
    step(hi_n, hi, a2, r3, a3, lambda p: (row, p * lo_n + lo, dp), sems[4], sems[5])
    grad = step(ndp, dp, a3, r4, None, lambda p: (row, col, p), sems[6], sems[7])

    me = (row * ncol + col) * ndp + dp
    skip = lax.rem(me * share, 128)
    place = (lax.broadcasted_iota(jnp.int32, (rows, 128), 0) * 128
             + lax.broadcasted_iota(jnp.int32, (rows, 128), 1))
    inside = jnp.logical_and(place >= skip, place < skip + share)
    momentum = mom_ref[...]
    weight = wgt_ref[...]
    mixed = beta_one * momentum + (1.0 - beta_one) * grad
    size = jnp.abs(mixed)
    part = jnp.sum(jnp.where(inside, size, 0.0), axis=0, keepdims=True)
    which = lax.broadcasted_iota(jnp.int32, (8, 128), 0)
    mine[...] = jnp.where(which == 0, part, jnp.where(which == 1, loss_ref[...], 0.0))
    plane, line = peers(sizes)
    exchange(nrow * ncol, lambda k: mine, rp, plane, sems[8], sems[9])
    total = mine[...]
    for k in range(nrow * ncol - 1):
        total = total + rp[k]
    line_sum[...] = total
    exchange(ndp, lambda k: line_sum, rl, line, sems[10], sems[11])
    for k in range(ndp - 1):
        total = total + rl[k]
    total_ref[...] = jnp.broadcast_to(jnp.sum(total, axis=1, keepdims=True), (8, 128))
    tau = jnp.sum(total[0:1, :], axis=1, keepdims=True) / params + 1e-06
    update = mixed / (size + tau)
    out_ref[0] = weight - learn_rate * (update + weight_decay * weight)
    out_ref[1] = beta_two * momentum + (1.0 - beta_two) * grad
    out_ref[2] = update


def lion_step(flat, loss_part, weights, momentum):
    sizes = tuple(lax.axis_size(a) for a in AXES)
    nrow, ncol, ndp = sizes
    count = nrow * ncol * ndp
    share = momentum.shape[0]
    params = weights.shape[0]
    rows = share_rows(share, count)
    me = lax.axis_index(AXES)
    skip = me * share % 128
    first = me * share // 128
    mom = lax.dynamic_update_slice(jnp.zeros((rows * 128,), jnp.float32), momentum, (skip,))
    spare = max(0, (count - 1) * share // 128 + rows - params // 128)
    wgt = jnp.pad(weights.reshape(-1, 128), ((0, spare), (0, 0)))
    wgt = lax.dynamic_slice_in_dim(wgt, first, rows, 0)
    lane0 = jnp.arange(128)[None, :] == 0
    loss_row = jnp.where(lane0, loss_part, 0.0)
    lo_n = split_col(ncol)
    hi_n = ncol // lo_n
    f32 = jnp.float32
    tail = (rows, 128)
    plane_n = nrow * ncol
    counts = (lo_n, nrow, hi_n, ndp, plane_n, ndp)
    sems = [pltpu.SemaphoreType.DMA((max(n - 1, 1),)) for n in counts for _ in range(2)]
    vmem = pl.BlockSpec(memory_space=pltpu.VMEM)

    def land(n, *rest):
        return pltpu.VMEM((max(n - 1, 1),) + rest + tail, f32)

    out, total = pl.pallas_call(
        lambda *refs: lion_kernel(sizes, share, params, *refs),
        out_shape=(jax.ShapeDtypeStruct((3,) + tail, f32), jax.ShapeDtypeStruct((8, 128), f32)),
        in_specs=[vmem] * 4,
        out_specs=(vmem, vmem),
        scratch_shapes=[
            pltpu.VMEM((lo_n, nrow, hi_n, ndp) + tail, f32),
            pltpu.VMEM((nrow, hi_n, ndp) + tail, f32), land(lo_n, nrow, hi_n, ndp),
            pltpu.VMEM((hi_n, ndp) + tail, f32), land(nrow, hi_n, ndp),
            pltpu.VMEM((ndp,) + tail, f32), land(hi_n, ndp),
            land(ndp),
            pltpu.VMEM((8, 128), f32), pltpu.VMEM((max(plane_n - 1, 1), 8, 128), f32),
            pltpu.VMEM((8, 128), f32), pltpu.VMEM((max(ndp - 1, 1), 8, 128), f32),
        ] + sems,
        compiler_params=pltpu.CompilerParams(
            collective_id=0, has_side_effects=True, vmem_limit_bytes=40 * 1024 * 1024),
    )(flat.reshape(-1, 128), loss_row, mom.reshape(rows, 128), wgt)
    out = lax.dynamic_slice_in_dim(out.reshape(3, rows * 128), skip, share, 1)
    return out[0], out[1], out[2], total[1, 0]


def directions():
    return [(-1, 0), (1, 0), (0, -1), (0, 1), (-1, -1), (1, -1), (-1, 1), (1, 1)]


def opposite(number):
    dr, dc = directions()[number]
    return directions().index((-dr, -dc))


SENT = (0, 1, 2, 3, 2, 2, 3, 3)


def near(sizes, number):
    nrow, ncol, _ = sizes
    dr, dc = directions()[number]
    row, col, dp = (lax.axis_index(a) for a in AXES)
    r, c = row + dr, col + dc
    there = jnp.logical_and(jnp.logical_and(r >= 0, r < nrow), jnp.logical_and(c >= 0, c < ncol))
    return there, (r, c, dp)


def dot(a, b):
    return lax.dot_general(a, b, (((1,), (0,)), ((), ())), preferred_element_type=jnp.float32)


def dot_t(a, b):
    return lax.dot_general(a, b, (((1,), (1,)), ((), ())), preferred_element_type=jnp.float32)


def bottleneck_kernel(
    sizes, height, tiles, x_ref, hot_ref, head_ref,
    wit1, af1, wot1, ab1, wo1, wit2, af2, wot2, ab2, wo2, wi2,
    gin1, gmid1, gout1, gin2, gmid2, gout2, ghead, loss_ref,
    s1, s2, d1, d2, z1, z2, h21, h22, y1, y2, sent, got, send_sem, recv_sem,
):
    f32, bf16 = jnp.float32, jnp.bfloat16
    lane = lax.broadcasted_iota(jnp.int32, (MID, 128), 1)
    step = 8 if height % 8 == 0 else height
    size = step * 128
    chunks = [slice(j * size, (j + 1) * size) for j in range(height // step)]
    own = slice(MID, 2 * MID)

    def inner(part):
        return slice(part.start + 128, part.stop + 128)

    got[...] = jnp.zeros_like(got)
    for z in (z1, z2):
        z[:, 0:256] = jnp.zeros((MID, 256), bf16)
        z[:, (height + 2) * 128 :] = jnp.zeros((MID, 256), bf16)
    barrier = pltpu.get_barrier_semaphore()
    for number in range(8):
        there, where = near(sizes, number)

        @pl.when(there)
        def _():
            pl.semaphore_signal(barrier, inc=1, device_id=where, device_id_type=MESH_ID)

    around = sum(near(sizes, number)[0].astype(jnp.int32) for number in range(8))
    pl.semaphore_wait(barrier, around)

    def copy(turn, number, slot):
        _, where = near(sizes, number)
        return pltpu.make_async_remote_copy(
            src_ref=sent.at[turn, SENT[number]], dst_ref=got.at[turn, slot],
            send_sem=send_sem.at[turn, number], recv_sem=recv_sem.at[turn, slot],
            device_id=where, device_id_type=MESH_ID)

    def rim_start(field, turn):
        sent[turn, 0] = field[own, 128:256]
        sent[turn, 1] = field[own, height * 128 : (height + 1) * 128]
        left = jnp.zeros((MID, 128), f32)
        right = jnp.zeros((MID, 128), f32)
        for y in range(1, height + 1):
            line = field[own, y * 128 : (y + 1) * 128].astype(f32)
            left = jnp.where(lane == y, pltpu.roll(line, y, 1), left)
            right = jnp.where(lane == y, pltpu.roll(line, (y + 1) % 128, 1), right)
        sent[turn, 2] = left.astype(bf16)
        sent[turn, 3] = right.astype(bf16)
        for number in range(8):
            there, _ = near(sizes, number)

            @pl.when(there)
            def _():
                copy(turn, number, opposite(number)).start()

    def rim_finish(field, turn):
        for number in range(8):
            there, _ = near(sizes, number)

            @pl.when(there)
            def _():
                copy(turn, number, opposite(number)).wait_send()
                copy(turn, number, number).wait_recv()

        field[own, 0:128] = got[turn, 0]
        field[own, (height + 1) * 128 :] = got[turn, 1]

        def column(side, low, high):
            low = pltpu.roll(got[turn, low].astype(f32), 128 - height, 1)
            high = pltpu.roll(got[turn, high].astype(f32), height, 1)
            middle = jnp.where(lane == height + 1, high, got[turn, side].astype(f32))
            return jnp.where(lane == 0, low, middle)

        left = column(2, 4, 5)
        right = column(3, 6, 7)
        for y in range(height + 2):
            part = slice(y * 128, (y + 1) * 128)
            line = field[own, part].astype(f32)
            before = jnp.where(lane == 0, left[:, y : y + 1], pltpu.roll(line, 1, 1))
            after = jnp.where(lane == 127, right[:, y : y + 1], pltpu.roll(line, 127, 1))
            field[0:MID, part] = before.astype(bf16)
            field[2 * MID :, part] = after.astype(bf16)

    def conv(w, field, part, reverse):
        wide = dot(w[...], field[:, part.start : part.stop + 256])
        total = None
        for r in range(3):
            at = (2 - r if reverse else r) * 128
            term = wide[r * MID : (r + 1) * MID, at : at + size]
            total = term if total is None else total + term
        return total

    def relu(value):
        return jnp.maximum(value, 0.0)

    for part in chunks:
        s1[own, inner(part)] = relu(dot(wit1[...], x_ref[:, part])).astype(bf16)
    rim_start(s1, 0)
    rim_finish(s1, 0)
    for part in chunks:
        h2 = relu(conv(af1, s1, part, False)).astype(bf16)
        h21[:, part] = h2
        y = relu(dot(wot1[...], h2) + x_ref[:, part].astype(f32)).astype(bf16)
        y1[:, part] = y
        s2[own, inner(part)] = relu(dot(wit2[...], y)).astype(bf16)
    rim_start(s2, 1)
    rim_finish(s2, 1)
    pool = jnp.zeros((C, 128), f32)
    for part in chunks:
        h2 = relu(conv(af2, s2, part, False)).astype(bf16)
        h22[:, part] = h2
        y = relu(dot(wot2[...], h2) + y1[:, part].astype(f32)).astype(bf16)
        y2[:, part] = y
        y = y.astype(f32)
        for k in range(step):
            pool = pool + y[:, k * 128 : (k + 1) * 128]

    wide_lane = lax.broadcasted_iota(jnp.int32, (C, 128), 1)
    one_lane = lax.broadcasted_iota(jnp.int32, (1, 128), 1)
    valid = one_lane < CLASSES
    head = head_ref[...]
    head_grad = jnp.zeros((C, 128), f32)
    upstream = jnp.zeros((C, 128), f32)
    loss = jnp.zeros((1, 1), f32)
    for t in range(128 // TILE_COLS):
        mine = wide_lane // TILE_COLS == t
        pooled = jnp.sum(jnp.where(mine, pool, 0.0), axis=1, keepdims=True) / (TILE_ROWS * TILE_COLS)
        logits = jnp.sum(pooled * head, axis=0, keepdims=True)
        highest = jnp.max(jnp.where(valid, logits, -jnp.inf), axis=1, keepdims=True)
        power = jnp.where(valid, jnp.exp(jnp.where(valid, logits - highest, 0.0)), 0.0)
        spread = jnp.sum(power, axis=1, keepdims=True)
        onehot = hot_ref[t : t + 1, :]
        loss = loss + jnp.log(spread) + highest - jnp.sum(onehot * logits, axis=1, keepdims=True)
        dlogits = (power / spread - onehot) / tiles
        head_grad = head_grad + pooled * dlogits
        dpool = jnp.sum(dlogits * head, axis=1, keepdims=True) / (TILE_ROWS * TILE_COLS)
        upstream = jnp.where(mine, dpool, upstream)
    ghead[...] = head_grad
    loss_ref[...] = jnp.broadcast_to(loss, (8, 128))
    upstream = upstream.astype(bf16).astype(f32)

    for part in chunks:
        for k in range(step):
            line = slice(part.start + k * 128, part.start + (k + 1) * 128)
            y2[:, line] = jnp.where(y2[:, line].astype(f32) > 0, upstream, 0.0).astype(bf16)
        dg2 = dot(wo2[...], y2[:, part])
        dg2 = jnp.where(h22[:, part].astype(f32) > 0, dg2, 0.0).astype(bf16)
        d2[own, inner(part)] = dg2
        z2[:, part.start + 256 : part.stop + 256] = dg2
    rim_start(d2, 2)
    gout2[...] = dot_t(h22[...], y2[...])

    def mid_grad(field, z):
        grid = [z[:, (2 - r) * 128 : (2 - r + height + 2) * 128] for r in range(3)]
        return dot_t(field[...], jnp.concatenate(grid, axis=0))

    gmid2[...] = mid_grad(s2, z2)
    rim_finish(d2, 2)
    grad = jnp.zeros((C, MID), f32)
    for part in chunks:
        dg1 = conv(ab2, d2, part, True)
        dg1 = jnp.where(s2[own, inner(part)].astype(f32) > 0, dg1, 0.0).astype(bf16)
        grad = grad + dot_t(y1[:, part], dg1)
        dy = (dot(wi2[...], dg1) + y2[:, part].astype(f32)).astype(bf16).astype(f32)
        dz = jnp.where(y1[:, part].astype(f32) > 0, dy, 0.0).astype(bf16)
        y2[:, part] = dz
        dg2 = dot(wo1[...], dz)
        dg2 = jnp.where(h21[:, part].astype(f32) > 0, dg2, 0.0).astype(bf16)
        d1[own, inner(part)] = dg2
        z1[:, part.start + 256 : part.stop + 256] = dg2
    gin2[...] = grad
    rim_start(d1, 3)
    gout1[...] = dot_t(h21[...], y2[...])
    gmid1[...] = mid_grad(s1, z1)
    rim_finish(d1, 3)
    grad = jnp.zeros((C, MID), f32)
    for part in chunks:
        dg1 = conv(ab1, d1, part, True)
        dg1 = jnp.where(s1[own, inner(part)].astype(f32) > 0, dg1, 0.0).astype(bf16)
        grad = grad + dot_t(x_ref[:, part], dg1)
    gin1[...] = grad


def local(image, labels, weights, momentum):
    sizes = tuple(lax.axis_size(a) for a in AXES)
    height, width = image.shape[2], image.shape[3]
    assert width == 128 and height == TILE_ROWS and height + 2 < 128
    f32, bf16 = jnp.float32, jnp.bfloat16
    blocks_list, head = unpack(weights)
    total_tiles = labels.shape[1] * labels.shape[2] * sizes[0] * sizes[1] * sizes[2]
    x = image[0].reshape(C, height * width)
    hot = labels[0, 0][:, None] == jnp.arange(128, dtype=jnp.int32)
    hot = jnp.pad(hot.astype(f32), ((0, 8 - hot.shape[0]), (0, 0)))
    head = jnp.pad(head, ((0, 0), (0, 128 - CLASSES)))
    packed = []
    for w_in, w_mid, w_out in blocks_list:
        taps = w_mid.reshape(3, 3, MID, MID)
        forth = taps.transpose(0, 3, 1, 2).reshape(3 * MID, 3 * MID)
        back = taps[:, ::-1].transpose(0, 2, 1, 3).reshape(3 * MID, 3 * MID)
        packed += [w_in.T, forth, w_out.T, back, w_out]
    packed.append(blocks_list[1][0])
    grads = [(C, MID), (3 * MID, 3 * MID), (MID, C)] * 2 + [(C, 128), (8, 128)]
    vmem = pl.BlockSpec(memory_space=pltpu.VMEM)
    wide = height * 128
    field = pltpu.VMEM((3 * MID, wide + 256), bf16)
    spaced = pltpu.VMEM((MID, wide + 512), bf16)
    slim = pltpu.VMEM((MID, wide), bf16)
    full = pltpu.VMEM((C, wide), bf16)
    gin1, gmid1, gout1, gin2, gmid2, gout2, ghead, loss = pl.pallas_call(
        lambda *refs: bottleneck_kernel(sizes, height, total_tiles, *refs),
        out_shape=[jax.ShapeDtypeStruct(g, f32) for g in grads],
        in_specs=[vmem] * (3 + len(packed)),
        out_specs=[vmem] * len(grads),
        scratch_shapes=[
            field, field, field, field, spaced, spaced, slim, slim, full, full,
            pltpu.VMEM((4, 4, MID, 128), bf16), pltpu.VMEM((4, 8, MID, 128), bf16),
            pltpu.SemaphoreType.DMA((4, 8)), pltpu.SemaphoreType.DMA((4, 8)),
        ],
        compiler_params=pltpu.CompilerParams(
            collective_id=1, has_side_effects=True, vmem_limit_bytes=48 * 1024 * 1024),
    )(x, hot, head, *packed)
    flat = []
    for gin, gmid, gout in ((gin1, gmid1, gout1), (gin2, gmid2, gout2)):
        gmid = gmid.reshape(3 * MID, 3, MID).transpose(1, 0, 2)
        flat += [gin.ravel(), gmid.ravel(), gout.ravel()]
    flat = jnp.concatenate(flat + [ghead[:, :CLASSES].ravel()])
    new_weights, new_momentum, update, loss_total = lion_step(flat, loss[0, 0], weights, momentum)
    return (new_weights, new_momentum, update, loss_total / total_tiles)


def solution(mesh):
    in_specs = (P("dp", None, "row", "col"), P("dp", "row", "col"), P(), P(("row", "col", "dp")))
    out_specs = (P(("row", "col", "dp")), P(("row", "col", "dp")), P(("row", "col", "dp")), P())
    return jax.shard_map(local, mesh=mesh, in_specs=in_specs, out_specs=out_specs, check_vma=False)
```

```python
import jax
import jax.numpy as jnp
from jax import lax
from jax.experimental import pallas as pl
from jax.experimental.pallas import tpu as pltpu
from jax.sharding import PartitionSpec as P

C = 256
MID = 64
CLASSES = 8
TILE_ROWS = 24
TILE_COLS = 64


beta_one = 0.9
beta_two = 0.99
learn_rate = 0.0001
weight_decay = 0.1


def unpack(weights):
    offset = 0
    blocks_list = []
    for number in range(2):
        w_in = weights[offset : offset + C * MID].reshape(C, MID)
        offset = offset + C * MID
        w_mid = weights[offset : offset + 9 * MID * MID].reshape(9, MID, MID)
        offset = offset + 9 * MID * MID
        w_out = weights[offset : offset + MID * C].reshape(MID, C)
        offset = offset + MID * C
        blocks_list.append(
            (w_in.astype(jnp.bfloat16), w_mid.astype(jnp.bfloat16), w_out.astype(jnp.bfloat16))
        )
    head = weights[offset:].reshape(C, CLASSES)
    return (blocks_list, head)


MESH_ID = pl.DeviceIdType.MESH
AXES = ("row", "col", "dp")


def share_rows(share, count):
    first = [d * share // 128 for d in range(count)]
    last = [-(-(d + 1) * share // 128) for d in range(count)]
    return max(b - a for a, b in zip(first, last))


def split_col(ncol):
    return 2 if ncol % 2 == 0 else 1


def peers(sizes):
    nrow, ncol, ndp = sizes
    row, col, dp = (lax.axis_index(a) for a in AXES)

    def plane(k):
        place = lax.rem(row * ncol + col + k, nrow * ncol)
        return (place // ncol, lax.rem(place, ncol), dp)

    def line(k):
        return (row, col, lax.rem(dp + k, ndp))

    return plane, line


def greet(sizes):
    nrow, ncol, ndp = sizes
    plane, line = peers(sizes)
    barrier = pltpu.get_barrier_semaphore()
    for target, count in ((plane, nrow * ncol), (line, ndp)):
        def one(k, carry, target=target):
            pl.semaphore_signal(barrier, inc=1, device_id=target(k), device_id_type=MESH_ID)
            return carry
        lax.fori_loop(1, count, one, 0)


def exchange(count, source, landing, target, send, recv):
    def copy(k):
        return pltpu.make_async_remote_copy(
            src_ref=source(k), dst_ref=landing.at[k - 1], send_sem=send.at[k - 1],
            recv_sem=recv.at[k - 1], device_id=target(k), device_id_type=MESH_ID)

    def start(k, carry):
        copy(k).start()
        return carry

    def finish(k, carry):
        copy(k).wait()
        return carry

    lax.fori_loop(1, count, start, 0)
    lax.fori_loop(1, count, finish, 0)


def lion_kernel(sizes, share, params, flat_ref, loss_ref, mom_ref, wgt_ref, out_ref, total_ref,
                held, a1, r1, a2, r2, r3, mine, rp, line_sum, rl, *sems):
    nrow, ncol, ndp = sizes
    lo_n = split_col(ncol)
    hi_n = ncol // lo_n
    rows = mom_ref.shape[0]
    row, col, dp = (lax.axis_index(a) for a in AXES)
    lo, hi = lax.rem(col, lo_n), col // lo_n
    greet(sizes)
    for r in range(nrow):
        for c in range(ncol):
            for z in range(ndp):
                start = ((r * ncol + c) * ndp + z) * share // 128
                have = min(rows, flat_ref.shape[0] - start)
                held[c % lo_n, r * hi_n + c // lo_n, z, 0:have] = flat_ref[start : start + have, :]
    pl.semaphore_wait(pltpu.get_barrier_semaphore(), nrow * ncol - 1 + ndp - 1)

    def step(count, me, now, landing, later, where, send, recv):
        exchange(count, lambda k: now.at[lax.rem(me + k, count)], landing,
                 lambda k: where(lax.rem(me + k, count)), send, recv)
        total = now[me]
        for k in range(count - 1):
            total = total + landing[k]
        if later is None:
            return total
        later[...] = total

    step(lo_n, lo, held, r1, a1, lambda p: (row, hi * lo_n + p, dp), sems[0], sems[1])
    step(nrow * hi_n, row * hi_n + hi, a1, r2, a2,
         lambda p: (p // hi_n, lax.rem(p, hi_n) * lo_n + lo, dp), sems[2], sems[3])
    grad = step(ndp, dp, a2, r3, None, lambda p: (row, col, p), sems[4], sems[5])

    me = (row * ncol + col) * ndp + dp
    skip = lax.rem(me * share, 128)
    place = (lax.broadcasted_iota(jnp.int32, (rows, 128), 0) * 128
             + lax.broadcasted_iota(jnp.int32, (rows, 128), 1))
    inside = jnp.logical_and(place >= skip, place < skip + share)
    momentum = mom_ref[...]
    weight = wgt_ref[...]
    mixed = beta_one * momentum + (1.0 - beta_one) * grad
    size = jnp.abs(mixed)
    part = jnp.sum(jnp.where(inside, size, 0.0), axis=0, keepdims=True)
    which = lax.broadcasted_iota(jnp.int32, (8, 128), 0)
    mine[...] = jnp.where(which == 0, part, jnp.where(which == 1, loss_ref[...], 0.0))
    plane, line = peers(sizes)
    exchange(nrow * ncol, lambda k: mine, rp, plane, sems[6], sems[7])
    total = mine[...]
    for k in range(nrow * ncol - 1):
        total = total + rp[k]
    line_sum[...] = total
    exchange(ndp, lambda k: line_sum, rl, line, sems[8], sems[9])
    for k in range(ndp - 1):
        total = total + rl[k]
    total_ref[...] = jnp.broadcast_to(jnp.sum(total, axis=1, keepdims=True), (8, 128))
    tau = jnp.sum(total[0:1, :], axis=1, keepdims=True) / params + 1e-06
    update = mixed / (size + tau)
    out_ref[0] = weight - learn_rate * (update + weight_decay * weight)
    out_ref[1] = beta_two * momentum + (1.0 - beta_two) * grad
    out_ref[2] = update


def lion_step(flat, loss_part, weights, momentum):
    sizes = tuple(lax.axis_size(a) for a in AXES)
    nrow, ncol, ndp = sizes
    count = nrow * ncol * ndp
    share = momentum.shape[0]
    params = weights.shape[0]
    rows = share_rows(share, count)
    me = lax.axis_index(AXES)
    skip = me * share % 128
    first = me * share // 128
    mom = lax.dynamic_update_slice(jnp.zeros((rows * 128,), jnp.float32), momentum, (skip,))
    spare = max(0, (count - 1) * share // 128 + rows - params // 128)
    wgt = jnp.pad(weights.reshape(-1, 128), ((0, spare), (0, 0)))
    wgt = lax.dynamic_slice_in_dim(wgt, first, rows, 0)
    lane0 = jnp.arange(128)[None, :] == 0
    loss_row = jnp.where(lane0, loss_part, 0.0)
    lo_n = split_col(ncol)
    hi_n = ncol // lo_n
    f32 = jnp.float32
    tail = (rows, 128)
    plane_n = nrow * ncol
    counts = (lo_n, nrow * hi_n, ndp, plane_n, ndp)
    sems = [pltpu.SemaphoreType.DMA((max(n - 1, 1),)) for n in counts for _ in range(2)]
    vmem = pl.BlockSpec(memory_space=pltpu.VMEM)

    def land(n, *rest):
        return pltpu.VMEM((max(n - 1, 1),) + rest + tail, f32)

    out, total = pl.pallas_call(
        lambda *refs: lion_kernel(sizes, share, params, *refs),
        out_shape=(jax.ShapeDtypeStruct((3,) + tail, f32), jax.ShapeDtypeStruct((8, 128), f32)),
        in_specs=[vmem] * 4,
        out_specs=(vmem, vmem),
        scratch_shapes=[
            pltpu.VMEM((lo_n, nrow * hi_n, ndp) + tail, f32),
            pltpu.VMEM((nrow * hi_n, ndp) + tail, f32), land(lo_n, nrow * hi_n, ndp),
            pltpu.VMEM((ndp,) + tail, f32), land(nrow * hi_n, ndp),
            land(ndp),
            pltpu.VMEM((8, 128), f32), pltpu.VMEM((max(plane_n - 1, 1), 8, 128), f32),
            pltpu.VMEM((8, 128), f32), pltpu.VMEM((max(ndp - 1, 1), 8, 128), f32),
        ] + sems,
        compiler_params=pltpu.CompilerParams(
            collective_id=0, has_side_effects=True, vmem_limit_bytes=40 * 1024 * 1024),
    )(flat.reshape(-1, 128), loss_row, mom.reshape(rows, 128), wgt)
    out = lax.dynamic_slice_in_dim(out.reshape(3, rows * 128), skip, share, 1)
    return out[0], out[1], out[2], total[1, 0]


def directions():
    return [(-1, 0), (1, 0), (0, -1), (0, 1), (-1, -1), (1, -1), (-1, 1), (1, 1)]


def opposite(number):
    dr, dc = directions()[number]
    return directions().index((-dr, -dc))


SENT = (0, 1, 2, 3, 2, 2, 3, 3)


def near(sizes, number):
    nrow, ncol, _ = sizes
    dr, dc = directions()[number]
    row, col, dp = (lax.axis_index(a) for a in AXES)
    r, c = row + dr, col + dc
    there = jnp.logical_and(jnp.logical_and(r >= 0, r < nrow), jnp.logical_and(c >= 0, c < ncol))
    return there, (r, c, dp)


def dot(a, b):
    return lax.dot_general(a, b, (((1,), (0,)), ((), ())), preferred_element_type=jnp.float32)


def dot_t(a, b):
    return lax.dot_general(a, b, (((1,), (1,)), ((), ())), preferred_element_type=jnp.float32)


def bottleneck_kernel(
    sizes, height, tiles, x_ref, hot_ref, head_ref,
    wit1, af1, wot1, ab1, wo1, wit2, af2, wot2, ab2, wo2, wi2,
    gin1, gmid1, gout1, gin2, gmid2, gout2, ghead, loss_ref,
    s1, s2, d1, d2, z1, z2, h21, h22, y1, y2, sent, got, send_sem, recv_sem,
):
    f32, bf16 = jnp.float32, jnp.bfloat16
    lane = lax.broadcasted_iota(jnp.int32, (MID, 128), 1)
    step = 8 if height % 8 == 0 else height
    size = step * 128
    chunks = [slice(j * size, (j + 1) * size) for j in range(height // step)]
    own = slice(MID, 2 * MID)

    def inner(part):
        return slice(part.start + 128, part.stop + 128)

    got[...] = jnp.zeros_like(got)
    for z in (z1, z2):
        z[:, 0:256] = jnp.zeros((MID, 256), bf16)
        z[:, (height + 2) * 128 :] = jnp.zeros((MID, 256), bf16)
    barrier = pltpu.get_barrier_semaphore()
    for number in range(8):
        there, where = near(sizes, number)

        @pl.when(there)
        def _():
            pl.semaphore_signal(barrier, inc=1, device_id=where, device_id_type=MESH_ID)

    around = sum(near(sizes, number)[0].astype(jnp.int32) for number in range(8))
    pl.semaphore_wait(barrier, around)

    def copy(turn, number, slot):
        _, where = near(sizes, number)
        return pltpu.make_async_remote_copy(
            src_ref=sent.at[turn, SENT[number]], dst_ref=got.at[turn, slot],
            send_sem=send_sem.at[turn, number], recv_sem=recv_sem.at[turn, slot],
            device_id=where, device_id_type=MESH_ID)

    def rim_start(field, turn):
        sent[turn, 0] = field[own, 128:256]
        sent[turn, 1] = field[own, height * 128 : (height + 1) * 128]
        left = jnp.zeros((MID, 128), f32)
        right = jnp.zeros((MID, 128), f32)
        for y in range(1, height + 1):
            line = field[own, y * 128 : (y + 1) * 128].astype(f32)
            left = jnp.where(lane == y, pltpu.roll(line, y, 1), left)
            right = jnp.where(lane == y, pltpu.roll(line, (y + 1) % 128, 1), right)
        sent[turn, 2] = left.astype(bf16)
        sent[turn, 3] = right.astype(bf16)
        for number in range(8):
            there, _ = near(sizes, number)

            @pl.when(there)
            def _():
                copy(turn, number, opposite(number)).start()

        for y in range(1, height + 1):
            part = slice(y * 128, (y + 1) * 128)
            line = field[own, part].astype(f32)
            field[0:MID, part] = pltpu.roll(line, 1, 1).astype(bf16)
            field[2 * MID :, part] = pltpu.roll(line, 127, 1).astype(bf16)

    def rim_finish(field, turn):
        for number in range(8):
            there, _ = near(sizes, number)

            @pl.when(there)
            def _():
                copy(turn, number, opposite(number)).wait_send()
                copy(turn, number, number).wait_recv()

        field[own, 0:128] = got[turn, 0]
        field[own, (height + 1) * 128 :] = got[turn, 1]

        def column(side, low, high):
            low = pltpu.roll(got[turn, low].astype(f32), 128 - height, 1)
            high = pltpu.roll(got[turn, high].astype(f32), height, 1)
            middle = jnp.where(lane == height + 1, high, got[turn, side].astype(f32))
            return jnp.where(lane == 0, low, middle)

        left = column(2, 4, 5)
        right = column(3, 6, 7)
        for y in range(height + 2):
            part = slice(y * 128, (y + 1) * 128)
            if y in (0, height + 1):
                line = field[own, part].astype(f32)
                before, after = pltpu.roll(line, 1, 1), pltpu.roll(line, 127, 1)
            else:
                before, after = field[0:MID, part].astype(f32), field[2 * MID :, part].astype(f32)
            before = jnp.where(lane == 0, left[:, y : y + 1], before)
            after = jnp.where(lane == 127, right[:, y : y + 1], after)
            field[0:MID, part] = before.astype(bf16)
            field[2 * MID :, part] = after.astype(bf16)

    def conv(w, field, part, reverse):
        wide = dot(w[...], field[:, part.start : part.stop + 256])
        total = None
        for r in range(3):
            at = (2 - r if reverse else r) * 128
            term = wide[r * MID : (r + 1) * MID, at : at + size]
            total = term if total is None else total + term
        return total

    def relu(value):
        return jnp.maximum(value, 0.0)

    for part in chunks:
        s1[own, inner(part)] = relu(dot(wit1[...], x_ref[:, part])).astype(bf16)
    rim_start(s1, 0)
    rim_finish(s1, 0)
    for part in chunks:
        h2 = relu(conv(af1, s1, part, False)).astype(bf16)
        h21[:, part] = h2
        y = relu(dot(wot1[...], h2) + x_ref[:, part].astype(f32)).astype(bf16)
        y1[:, part] = y
        s2[own, inner(part)] = relu(dot(wit2[...], y)).astype(bf16)
    rim_start(s2, 1)
    rim_finish(s2, 1)
    pool = jnp.zeros((C, 128), f32)
    for part in chunks:
        h2 = relu(conv(af2, s2, part, False)).astype(bf16)
        h22[:, part] = h2
        y = relu(dot(wot2[...], h2) + y1[:, part].astype(f32)).astype(bf16)
        y2[:, part] = y
        y = y.astype(f32)
        for k in range(step):
            pool = pool + y[:, k * 128 : (k + 1) * 128]

    wide_lane = lax.broadcasted_iota(jnp.int32, (C, 128), 1)
    one_lane = lax.broadcasted_iota(jnp.int32, (1, 128), 1)
    valid = one_lane < CLASSES
    head = head_ref[...]
    head_grad = jnp.zeros((C, 128), f32)
    upstream = jnp.zeros((C, 128), f32)
    loss = jnp.zeros((1, 1), f32)
    for t in range(128 // TILE_COLS):
        mine = wide_lane // TILE_COLS == t
        pooled = jnp.sum(jnp.where(mine, pool, 0.0), axis=1, keepdims=True) / (TILE_ROWS * TILE_COLS)
        logits = jnp.sum(pooled * head, axis=0, keepdims=True)
        highest = jnp.max(jnp.where(valid, logits, -jnp.inf), axis=1, keepdims=True)
        power = jnp.where(valid, jnp.exp(jnp.where(valid, logits - highest, 0.0)), 0.0)
        spread = jnp.sum(power, axis=1, keepdims=True)
        onehot = hot_ref[t : t + 1, :]
        loss = loss + jnp.log(spread) + highest - jnp.sum(onehot * logits, axis=1, keepdims=True)
        dlogits = (power / spread - onehot) / tiles
        head_grad = head_grad + pooled * dlogits
        dpool = jnp.sum(dlogits * head, axis=1, keepdims=True) / (TILE_ROWS * TILE_COLS)
        upstream = jnp.where(mine, dpool, upstream)
    ghead[...] = head_grad
    loss_ref[...] = jnp.broadcast_to(loss, (8, 128))
    upstream = upstream.astype(bf16).astype(f32)

    for part in chunks:
        for k in range(step):
            line = slice(part.start + k * 128, part.start + (k + 1) * 128)
            y2[:, line] = jnp.where(y2[:, line].astype(f32) > 0, upstream, 0.0).astype(bf16)
        dg2 = dot(wo2[...], y2[:, part])
        dg2 = jnp.where(h22[:, part].astype(f32) > 0, dg2, 0.0).astype(bf16)
        d2[own, inner(part)] = dg2
        z2[:, part.start + 256 : part.stop + 256] = dg2
    rim_start(d2, 2)
    gout2[...] = dot_t(h22[...], y2[...])

    def mid_grad(field, z):
        grid = [z[:, (2 - r) * 128 : (2 - r + height + 2) * 128] for r in range(3)]
        return dot_t(field[...], jnp.concatenate(grid, axis=0))

    gmid2[...] = mid_grad(s2, z2)
    rim_finish(d2, 2)
    grad = jnp.zeros((C, MID), f32)
    for part in chunks:
        dg1 = conv(ab2, d2, part, True)
        dg1 = jnp.where(s2[own, inner(part)].astype(f32) > 0, dg1, 0.0).astype(bf16)
        grad = grad + dot_t(y1[:, part], dg1)
        dy = (dot(wi2[...], dg1) + y2[:, part].astype(f32)).astype(bf16).astype(f32)
        dz = jnp.where(y1[:, part].astype(f32) > 0, dy, 0.0).astype(bf16)
        y2[:, part] = dz
        dg2 = dot(wo1[...], dz)
        dg2 = jnp.where(h21[:, part].astype(f32) > 0, dg2, 0.0).astype(bf16)
        d1[own, inner(part)] = dg2
        z1[:, part.start + 256 : part.stop + 256] = dg2
    gin2[...] = grad
    rim_start(d1, 3)
    gout1[...] = dot_t(h21[...], y2[...])
    gmid1[...] = mid_grad(s1, z1)
    rim_finish(d1, 3)
    grad = jnp.zeros((C, MID), f32)
    for part in chunks:
        dg1 = conv(ab1, d1, part, True)
        dg1 = jnp.where(s1[own, inner(part)].astype(f32) > 0, dg1, 0.0).astype(bf16)
        grad = grad + dot_t(x_ref[:, part], dg1)
    gin1[...] = grad


def local(image, labels, weights, momentum):
    sizes = tuple(lax.axis_size(a) for a in AXES)
    height, width = image.shape[2], image.shape[3]
    assert width == 128 and height == TILE_ROWS and height + 2 < 128
    f32, bf16 = jnp.float32, jnp.bfloat16
    blocks_list, head = unpack(weights)
    total_tiles = labels.shape[1] * labels.shape[2] * sizes[0] * sizes[1] * sizes[2]
    x = image[0].reshape(C, height * width)
    hot = labels[0, 0][:, None] == jnp.arange(128, dtype=jnp.int32)
    hot = jnp.pad(hot.astype(f32), ((0, 8 - hot.shape[0]), (0, 0)))
    head = jnp.pad(head, ((0, 0), (0, 128 - CLASSES)))
    packed = []
    for w_in, w_mid, w_out in blocks_list:
        taps = w_mid.reshape(3, 3, MID, MID)
        forth = taps.transpose(0, 3, 1, 2).reshape(3 * MID, 3 * MID)
        back = taps[:, ::-1].transpose(0, 2, 1, 3).reshape(3 * MID, 3 * MID)
        packed += [w_in.T, forth, w_out.T, back, w_out]
    packed.append(blocks_list[1][0])
    grads = [(C, MID), (3 * MID, 3 * MID), (MID, C)] * 2 + [(C, 128), (8, 128)]
    vmem = pl.BlockSpec(memory_space=pltpu.VMEM)
    wide = height * 128
    field = pltpu.VMEM((3 * MID, wide + 256), bf16)
    spaced = pltpu.VMEM((MID, wide + 512), bf16)
    slim = pltpu.VMEM((MID, wide), bf16)
    full = pltpu.VMEM((C, wide), bf16)
    gin1, gmid1, gout1, gin2, gmid2, gout2, ghead, loss = pl.pallas_call(
        lambda *refs: bottleneck_kernel(sizes, height, total_tiles, *refs),
        out_shape=[jax.ShapeDtypeStruct(g, f32) for g in grads],
        in_specs=[vmem] * (3 + len(packed)),
        out_specs=[vmem] * len(grads),
        scratch_shapes=[
            field, field, field, field, spaced, spaced, slim, slim, full, full,
            pltpu.VMEM((4, 4, MID, 128), bf16), pltpu.VMEM((4, 8, MID, 128), bf16),
            pltpu.SemaphoreType.DMA((4, 8)), pltpu.SemaphoreType.DMA((4, 8)),
        ],
        compiler_params=pltpu.CompilerParams(
            collective_id=1, has_side_effects=True, vmem_limit_bytes=48 * 1024 * 1024),
    )(x, hot, head, *packed)
    flat = []
    for gin, gmid, gout in ((gin1, gmid1, gout1), (gin2, gmid2, gout2)):
        gmid = gmid.reshape(3 * MID, 3, MID).transpose(1, 0, 2)
        flat += [gin.ravel(), gmid.ravel(), gout.ravel()]
    flat = jnp.concatenate(flat + [ghead[:, :CLASSES].ravel()])
    new_weights, new_momentum, update, loss_total = lion_step(flat, loss[0, 0], weights, momentum)
    return (new_weights, new_momentum, update, loss_total / total_tiles)


def solution(mesh):
    in_specs = (P("dp", None, "row", "col"), P("dp", "row", "col"), P(), P(("row", "col", "dp")))
    out_specs = (P(("row", "col", "dp")), P(("row", "col", "dp")), P(("row", "col", "dp")), P())
    return jax.shard_map(local, mesh=mesh, in_specs=in_specs, out_specs=out_specs, check_vma=False)
```

```python
import jax
import jax.numpy as jnp
from jax import lax
from jax.experimental import pallas as pl
from jax.experimental.pallas import tpu as pltpu
from jax.sharding import PartitionSpec as P

C = 256
MID = 64
CLASSES = 8
TILE_ROWS = 24
TILE_COLS = 64


beta_one = 0.9
beta_two = 0.99
learn_rate = 0.0001
weight_decay = 0.1


def unpack(weights):
    offset = 0
    blocks_list = []
    for number in range(2):
        w_in = weights[offset : offset + C * MID].reshape(C, MID)
        offset = offset + C * MID
        w_mid = weights[offset : offset + 9 * MID * MID].reshape(9, MID, MID)
        offset = offset + 9 * MID * MID
        w_out = weights[offset : offset + MID * C].reshape(MID, C)
        offset = offset + MID * C
        blocks_list.append(
            (w_in.astype(jnp.bfloat16), w_mid.astype(jnp.bfloat16), w_out.astype(jnp.bfloat16))
        )
    head = weights[offset:].reshape(C, CLASSES)
    return (blocks_list, head)


MESH_ID = pl.DeviceIdType.MESH
AXES = ("row", "col", "dp")


def share_rows(share, count):
    first = [d * share // 128 for d in range(count)]
    last = [-(-(d + 1) * share // 128) for d in range(count)]
    return max(b - a for a, b in zip(first, last))


def split_col(ncol):
    return 2 if ncol % 2 == 0 else 1


def peers(sizes):
    nrow, ncol, ndp = sizes
    row, col, dp = (lax.axis_index(a) for a in AXES)

    def plane(k):
        place = lax.rem(row * ncol + col + k, nrow * ncol)
        return (place // ncol, lax.rem(place, ncol), dp)

    def line(k):
        return (row, col, lax.rem(dp + k, ndp))

    return plane, line


def each(count, body):
    if count <= 8:
        for k in range(1, count):
            body(k, 0)
    else:
        lax.fori_loop(1, count, body, 0)


def greet(sizes):
    nrow, ncol, ndp = sizes
    plane, line = peers(sizes)
    barrier = pltpu.get_barrier_semaphore()
    for target, count in ((plane, nrow * ncol), (line, ndp)):
        def one(k, carry, target=target):
            pl.semaphore_signal(barrier, inc=1, device_id=target(k), device_id_type=MESH_ID)
            return carry
        each(count, one)


def exchange(count, source, landing, target, send, recv):
    def copy(k):
        return pltpu.make_async_remote_copy(
            src_ref=source(k), dst_ref=landing.at[k - 1], send_sem=send.at[k - 1],
            recv_sem=recv.at[k - 1], device_id=target(k), device_id_type=MESH_ID)

    def start(k, carry):
        copy(k).start()
        return carry

    def finish(k, carry):
        copy(k).wait()
        return carry

    each(count, start)
    each(count, finish)


def lion_kernel(sizes, share, params, flat_ref, loss_ref, mom_ref, wgt_ref, out_ref, total_ref,
                held, a1, r1, a2, r2, r3, mine, rp, line_sum, rl, *sems):
    nrow, ncol, ndp = sizes
    lo_n = split_col(ncol)
    hi_n = ncol // lo_n
    rows = mom_ref.shape[0]
    row, col, dp = (lax.axis_index(a) for a in AXES)
    lo, hi = lax.rem(col, lo_n), col // lo_n
    greet(sizes)
    for r in range(nrow):
        for c in range(ncol):
            for z in range(ndp):
                start = ((r * ncol + c) * ndp + z) * share // 128
                have = min(rows, flat_ref.shape[0] - start)
                held[c % lo_n, r * hi_n + c // lo_n, z, 0:have] = flat_ref[start : start + have, :]
    pl.semaphore_wait(pltpu.get_barrier_semaphore(), nrow * ncol - 1 + ndp - 1)

    def step(count, me, now, landing, later, where, send, recv):
        exchange(count, lambda k: now.at[lax.rem(me + k, count)], landing,
                 lambda k: where(lax.rem(me + k, count)), send, recv)
        total = now[me]
        for k in range(count - 1):
            total = total + landing[k]
        if later is None:
            return total
        later[...] = total

    step(lo_n, lo, held, r1, a1, lambda p: (row, hi * lo_n + p, dp), sems[0], sems[1])
    step(nrow * hi_n, row * hi_n + hi, a1, r2, a2,
         lambda p: (p // hi_n, lax.rem(p, hi_n) * lo_n + lo, dp), sems[2], sems[3])
    grad = step(ndp, dp, a2, r3, None, lambda p: (row, col, p), sems[4], sems[5])

    me = (row * ncol + col) * ndp + dp
    skip = lax.rem(me * share, 128)
    place = (lax.broadcasted_iota(jnp.int32, (rows, 128), 0) * 128
             + lax.broadcasted_iota(jnp.int32, (rows, 128), 1))
    inside = jnp.logical_and(place >= skip, place < skip + share)
    momentum = mom_ref[...]
    weight = wgt_ref[...]
    mixed = beta_one * momentum + (1.0 - beta_one) * grad
    size = jnp.abs(mixed)
    part = jnp.sum(jnp.where(inside, size, 0.0), axis=0, keepdims=True)
    which = lax.broadcasted_iota(jnp.int32, (8, 128), 0)
    at_loss = jnp.logical_and(which == 1, lax.broadcasted_iota(jnp.int32, (8, 128), 1) == 0)
    mine[...] = jnp.where(which == 0, part, jnp.where(at_loss, loss_ref[...], 0.0))
    plane, line = peers(sizes)
    exchange(nrow * ncol, lambda k: mine, rp, plane, sems[6], sems[7])
    total = mine[...]
    for k in range(nrow * ncol - 1):
        total = total + rp[k]
    line_sum[...] = total
    exchange(ndp, lambda k: line_sum, rl, line, sems[8], sems[9])
    for k in range(ndp - 1):
        total = total + rl[k]
    total_ref[...] = jnp.broadcast_to(jnp.sum(total, axis=1, keepdims=True), (8, 128))
    tau = jnp.sum(total[0:1, :], axis=1, keepdims=True) / params + 1e-06
    update = mixed / (size + tau)
    out_ref[0] = weight - learn_rate * (update + weight_decay * weight)
    out_ref[1] = beta_two * momentum + (1.0 - beta_two) * grad
    out_ref[2] = update


def lion_step(flat, loss_part, weights, momentum):
    sizes = tuple(lax.axis_size(a) for a in AXES)
    nrow, ncol, ndp = sizes
    count = nrow * ncol * ndp
    share = momentum.shape[0]
    params = weights.shape[0]
    rows = share_rows(share, count)
    me = lax.axis_index(AXES)
    skip = me * share % 128
    first = me * share // 128
    mom = lax.dynamic_update_slice(jnp.zeros((rows * 128,), jnp.float32), momentum, (skip,))
    spare = max(0, (count - 1) * share // 128 + rows - params // 128)
    wgt = jnp.pad(weights.reshape(-1, 128), ((0, spare), (0, 0)))
    wgt = lax.dynamic_slice_in_dim(wgt, first, rows, 0)
    lo_n = split_col(ncol)
    hi_n = ncol // lo_n
    f32 = jnp.float32
    tail = (rows, 128)
    plane_n = nrow * ncol
    counts = (lo_n, nrow * hi_n, ndp, plane_n, ndp)
    sems = [pltpu.SemaphoreType.DMA((max(n - 1, 1),)) for n in counts for _ in range(2)]
    vmem = pl.BlockSpec(memory_space=pltpu.VMEM)

    def land(n, *rest):
        return pltpu.VMEM((max(n - 1, 1),) + rest + tail, f32)

    out, total = pl.pallas_call(
        lambda *refs: lion_kernel(sizes, share, params, *refs),
        out_shape=(jax.ShapeDtypeStruct((3,) + tail, f32), jax.ShapeDtypeStruct((8, 128), f32)),
        in_specs=[vmem] * 4,
        out_specs=(vmem, vmem),
        scratch_shapes=[
            pltpu.VMEM((lo_n, nrow * hi_n, ndp) + tail, f32),
            pltpu.VMEM((nrow * hi_n, ndp) + tail, f32), land(lo_n, nrow * hi_n, ndp),
            pltpu.VMEM((ndp,) + tail, f32), land(nrow * hi_n, ndp),
            land(ndp),
            pltpu.VMEM((8, 128), f32), pltpu.VMEM((max(plane_n - 1, 1), 8, 128), f32),
            pltpu.VMEM((8, 128), f32), pltpu.VMEM((max(ndp - 1, 1), 8, 128), f32),
        ] + sems,
        compiler_params=pltpu.CompilerParams(
            collective_id=0, has_side_effects=True, vmem_limit_bytes=40 * 1024 * 1024),
    )(flat.reshape(-1, 128), loss_part, mom.reshape(rows, 128), wgt)
    out = lax.dynamic_slice_in_dim(out.reshape(3, rows * 128), skip, share, 1)
    return out[0], out[1], out[2], total[1, 0]


def directions():
    return [(-1, 0), (1, 0), (0, -1), (0, 1), (-1, -1), (1, -1), (-1, 1), (1, 1)]


def opposite(number):
    dr, dc = directions()[number]
    return directions().index((-dr, -dc))


SENT = (0, 1, 2, 3, 2, 2, 3, 3)


def near(sizes, number):
    nrow, ncol, _ = sizes
    dr, dc = directions()[number]
    row, col, dp = (lax.axis_index(a) for a in AXES)
    r, c = row + dr, col + dc
    there = jnp.logical_and(jnp.logical_and(r >= 0, r < nrow), jnp.logical_and(c >= 0, c < ncol))
    return there, (r, c, dp)


def dot(a, b):
    return lax.dot_general(a, b, (((1,), (0,)), ((), ())), preferred_element_type=jnp.float32)


def dot_t(a, b):
    return lax.dot_general(a, b, (((1,), (1,)), ((), ())), preferred_element_type=jnp.float32)


def bottleneck_kernel(
    sizes, height, tiles, x_ref, hot_ref, head_ref,
    wit1, af1, wot1, ab1, wo1, wit2, af2, wot2, ab2, wo2, wi2,
    gin1, gmid1, gout1, gin2, gmid2, gout2, ghead, loss_ref,
    s1, s2, d1, d2, z1, z2, h21, h22, y1, y2, sent, got, send_sem, recv_sem,
):
    f32, bf16 = jnp.float32, jnp.bfloat16
    lane = lax.broadcasted_iota(jnp.int32, (MID, 128), 1)
    step = 8 if height % 8 == 0 else height
    size = step * 128
    chunks = [slice(j * size, (j + 1) * size) for j in range(height // step)]
    own = slice(MID, 2 * MID)

    def inner(part):
        return slice(part.start + 128, part.stop + 128)

    got[...] = jnp.zeros_like(got)
    for z in (z1, z2):
        z[:, 0:256] = jnp.zeros((MID, 256), bf16)
        z[:, (height + 2) * 128 :] = jnp.zeros((MID, 256), bf16)
    barrier = pltpu.get_barrier_semaphore()
    for number in range(8):
        there, where = near(sizes, number)

        @pl.when(there)
        def _():
            pl.semaphore_signal(barrier, inc=1, device_id=where, device_id_type=MESH_ID)

    around = sum(near(sizes, number)[0].astype(jnp.int32) for number in range(8))
    pl.semaphore_wait(barrier, around)

    def copy(turn, number, slot):
        _, where = near(sizes, number)
        return pltpu.make_async_remote_copy(
            src_ref=sent.at[turn, SENT[number]], dst_ref=got.at[turn, slot],
            send_sem=send_sem.at[turn, number], recv_sem=recv_sem.at[turn, slot],
            device_id=where, device_id_type=MESH_ID)

    def rim_start(field, turn):
        sent[turn, 0] = field[own, 128:256]
        sent[turn, 1] = field[own, height * 128 : (height + 1) * 128]
        left = jnp.zeros((MID, 128), f32)
        right = jnp.zeros((MID, 128), f32)
        for y in range(1, height + 1):
            line = field[own, y * 128 : (y + 1) * 128].astype(f32)
            left = jnp.where(lane == y, pltpu.roll(line, y, 1), left)
            right = jnp.where(lane == y, pltpu.roll(line, (y + 1) % 128, 1), right)
        sent[turn, 2] = left.astype(bf16)
        sent[turn, 3] = right.astype(bf16)
        for number in range(8):
            there, _ = near(sizes, number)

            @pl.when(there)
            def _():
                copy(turn, number, opposite(number)).start()

        for y in range(1, height + 1):
            part = slice(y * 128, (y + 1) * 128)
            line = field[own, part].astype(f32)
            field[0:MID, part] = pltpu.roll(line, 1, 1).astype(bf16)
            field[2 * MID :, part] = pltpu.roll(line, 127, 1).astype(bf16)

    def rim_finish(field, turn):
        for number in range(8):
            there, _ = near(sizes, number)

            @pl.when(there)
            def _():
                copy(turn, number, opposite(number)).wait_send()
                copy(turn, number, number).wait_recv()

        field[own, 0:128] = got[turn, 0]
        field[own, (height + 1) * 128 :] = got[turn, 1]

        def column(side, low, high):
            low = pltpu.roll(got[turn, low].astype(f32), 128 - height, 1)
            high = pltpu.roll(got[turn, high].astype(f32), height, 1)
            middle = jnp.where(lane == height + 1, high, got[turn, side].astype(f32))
            return jnp.where(lane == 0, low, middle)

        left = column(2, 4, 5)
        right = column(3, 6, 7)
        for y in range(height + 2):
            part = slice(y * 128, (y + 1) * 128)
            if y in (0, height + 1):
                line = field[own, part].astype(f32)
                before, after = pltpu.roll(line, 1, 1), pltpu.roll(line, 127, 1)
            else:
                before, after = field[0:MID, part].astype(f32), field[2 * MID :, part].astype(f32)
            before = jnp.where(lane == 0, left[:, y : y + 1], before)
            after = jnp.where(lane == 127, right[:, y : y + 1], after)
            field[0:MID, part] = before.astype(bf16)
            field[2 * MID :, part] = after.astype(bf16)

    def conv(w, field, part, reverse):
        wide = dot(w[...], field[:, part.start : part.stop + 256])
        total = None
        for r in range(3):
            at = (2 - r if reverse else r) * 128
            term = wide[r * MID : (r + 1) * MID, at : at + size]
            total = term if total is None else total + term
        return total

    def relu(value):
        return jnp.maximum(value, 0.0)

    for part in chunks:
        s1[own, inner(part)] = relu(dot(wit1[...], x_ref[:, part])).astype(bf16)
    rim_start(s1, 0)
    rim_finish(s1, 0)
    for part in chunks:
        h2 = relu(conv(af1, s1, part, False)).astype(bf16)
        h21[:, part] = h2
        y = relu(dot(wot1[...], h2) + x_ref[:, part].astype(f32)).astype(bf16)
        y1[:, part] = y
        s2[own, inner(part)] = relu(dot(wit2[...], y)).astype(bf16)
    rim_start(s2, 1)
    rim_finish(s2, 1)
    pool = jnp.zeros((C, 128), f32)
    for part in chunks:
        h2 = relu(conv(af2, s2, part, False)).astype(bf16)
        h22[:, part] = h2
        y = relu(dot(wot2[...], h2) + y1[:, part].astype(f32)).astype(bf16)
        y2[:, part] = y
        y = y.astype(f32)
        for k in range(step):
            pool = pool + y[:, k * 128 : (k + 1) * 128]

    wide_lane = lax.broadcasted_iota(jnp.int32, (C, 128), 1)
    one_lane = lax.broadcasted_iota(jnp.int32, (1, 128), 1)
    valid = one_lane < CLASSES
    head = head_ref[...]
    head_grad = jnp.zeros((C, 128), f32)
    upstream = jnp.zeros((C, 128), f32)
    loss = jnp.zeros((1, 1), f32)
    for t in range(128 // TILE_COLS):
        mine = wide_lane // TILE_COLS == t
        pooled = jnp.sum(jnp.where(mine, pool, 0.0), axis=1, keepdims=True) / (TILE_ROWS * TILE_COLS)
        logits = jnp.sum(pooled * head, axis=0, keepdims=True)
        highest = jnp.max(jnp.where(valid, logits, -jnp.inf), axis=1, keepdims=True)
        power = jnp.where(valid, jnp.exp(jnp.where(valid, logits - highest, 0.0)), 0.0)
        spread = jnp.sum(power, axis=1, keepdims=True)
        onehot = hot_ref[t : t + 1, :]
        loss = loss + jnp.log(spread) + highest - jnp.sum(onehot * logits, axis=1, keepdims=True)
        dlogits = (power / spread - onehot) / tiles
        head_grad = head_grad + pooled * dlogits
        dpool = jnp.sum(dlogits * head, axis=1, keepdims=True) / (TILE_ROWS * TILE_COLS)
        upstream = jnp.where(mine, dpool, upstream)
    ghead[...] = head_grad
    loss_ref[...] = jnp.broadcast_to(loss, (8, 128))
    upstream = upstream.astype(bf16).astype(f32)

    for part in chunks:
        for k in range(step):
            line = slice(part.start + k * 128, part.start + (k + 1) * 128)
            y2[:, line] = jnp.where(y2[:, line].astype(f32) > 0, upstream, 0.0).astype(bf16)
        dg2 = dot(wo2[...], y2[:, part])
        dg2 = jnp.where(h22[:, part].astype(f32) > 0, dg2, 0.0).astype(bf16)
        d2[own, inner(part)] = dg2
        z2[:, part.start + 256 : part.stop + 256] = dg2
    rim_start(d2, 2)
    gout2[...] = dot_t(h22[...], y2[...])

    def mid_grad(field, z):
        grid = [z[:, (2 - r) * 128 : (2 - r + height + 2) * 128] for r in range(3)]
        return dot_t(field[...], jnp.concatenate(grid, axis=0))

    gmid2[...] = mid_grad(s2, z2)
    rim_finish(d2, 2)
    grad = jnp.zeros((C, MID), f32)
    for part in chunks:
        dg1 = conv(ab2, d2, part, True)
        dg1 = jnp.where(s2[own, inner(part)].astype(f32) > 0, dg1, 0.0).astype(bf16)
        grad = grad + dot_t(y1[:, part], dg1)
        dy = (dot(wi2[...], dg1) + y2[:, part].astype(f32)).astype(bf16).astype(f32)
        dz = jnp.where(y1[:, part].astype(f32) > 0, dy, 0.0).astype(bf16)
        y2[:, part] = dz
        dg2 = dot(wo1[...], dz)
        dg2 = jnp.where(h21[:, part].astype(f32) > 0, dg2, 0.0).astype(bf16)
        d1[own, inner(part)] = dg2
        z1[:, part.start + 256 : part.stop + 256] = dg2
    gin2[...] = grad
    rim_start(d1, 3)
    gout1[...] = dot_t(h21[...], y2[...])
    gmid1[...] = mid_grad(s1, z1)
    rim_finish(d1, 3)
    grad = jnp.zeros((C, MID), f32)
    for part in chunks:
        dg1 = conv(ab1, d1, part, True)
        dg1 = jnp.where(s1[own, inner(part)].astype(f32) > 0, dg1, 0.0).astype(bf16)
        grad = grad + dot_t(x_ref[:, part], dg1)
    gin1[...] = grad


def local(image, labels, weights, momentum):
    sizes = tuple(lax.axis_size(a) for a in AXES)
    height, width = image.shape[2], image.shape[3]
    assert width == 128 and height == TILE_ROWS and height + 2 < 128
    f32, bf16 = jnp.float32, jnp.bfloat16
    blocks_list, head = unpack(weights)
    total_tiles = labels.shape[1] * labels.shape[2] * sizes[0] * sizes[1] * sizes[2]
    x = image[0].reshape(C, height * width)
    hot = labels[0, 0][:, None] == jnp.arange(128, dtype=jnp.int32)
    hot = jnp.pad(hot.astype(f32), ((0, 8 - hot.shape[0]), (0, 0)))
    head = jnp.pad(head, ((0, 0), (0, 128 - CLASSES)))
    packed = []
    for w_in, w_mid, w_out in blocks_list:
        taps = w_mid.reshape(3, 3, MID, MID)
        forth = taps.transpose(0, 3, 1, 2).reshape(3 * MID, 3 * MID)
        back = taps[:, ::-1].transpose(0, 2, 1, 3).reshape(3 * MID, 3 * MID)
        packed += [w_in.T, forth, w_out.T, back, w_out]
    packed.append(blocks_list[1][0])
    grads = [(C, MID), (3 * MID, 3 * MID), (MID, C)] * 2 + [(C, 128), (8, 128)]
    vmem = pl.BlockSpec(memory_space=pltpu.VMEM)
    wide = height * 128
    field = pltpu.VMEM((3 * MID, wide + 256), bf16)
    spaced = pltpu.VMEM((MID, wide + 512), bf16)
    slim = pltpu.VMEM((MID, wide), bf16)
    full = pltpu.VMEM((C, wide), bf16)
    gin1, gmid1, gout1, gin2, gmid2, gout2, ghead, loss = pl.pallas_call(
        lambda *refs: bottleneck_kernel(sizes, height, total_tiles, *refs),
        out_shape=[jax.ShapeDtypeStruct(g, f32) for g in grads],
        in_specs=[vmem] * (3 + len(packed)),
        out_specs=[vmem] * len(grads),
        scratch_shapes=[
            field, field, field, field, spaced, spaced, slim, slim, full, full,
            pltpu.VMEM((4, 4, MID, 128), bf16), pltpu.VMEM((4, 8, MID, 128), bf16),
            pltpu.SemaphoreType.DMA((4, 8)), pltpu.SemaphoreType.DMA((4, 8)),
        ],
        compiler_params=pltpu.CompilerParams(
            collective_id=1, has_side_effects=True, vmem_limit_bytes=48 * 1024 * 1024),
    )(x, hot, head, *packed)
    flat = []
    for gin, gmid, gout in ((gin1, gmid1, gout1), (gin2, gmid2, gout2)):
        gmid = gmid.reshape(3 * MID, 3, MID).transpose(1, 0, 2)
        flat += [gin.ravel(), gmid.ravel(), gout.ravel()]
    flat = jnp.concatenate(flat + [ghead[:, :CLASSES].ravel()])
    new_weights, new_momentum, update, loss_total = lion_step(flat, loss, weights, momentum)
    return (new_weights, new_momentum, update, loss_total / total_tiles)


def solution(mesh):
    in_specs = (P("dp", None, "row", "col"), P("dp", "row", "col"), P(), P(("row", "col", "dp")))
    out_specs = (P(("row", "col", "dp")), P(("row", "col", "dp")), P(("row", "col", "dp")), P())
    return jax.shard_map(local, mesh=mesh, in_specs=in_specs, out_specs=out_specs, check_vma=False)
```
